32 devices in a mesh: pts: 8 (over z, y), ch: 4 (over x, core).
Axes of the slice: x: 2, y: 2, z: 4, core: 2. Of those that a mesh axis runs over, the one named last changes fastest.
Arguments:
- points_in: bfloat16 [4096, 256], P('pts'), may hold values from -6 to 6
- neighbor_offsets: int32 [4096, 16], P('pts'), may hold values from -128 to 128, as said below
- kernel_ids: int32 [4096, 16], P('pts'), may hold values from 0 to 26
- cluster_ids: int32 [4096], P('pts'), may hold values from 0 to 1023, as said below
- owners: int32 [4096], P('pts'), may hold values from 0 to 7, as said below
- conv_weight: bfloat16 [27, 256], replicated, may hold values from -1.5 to 1.5
- norm_gain: float32 [256], replicated, may hold values from 0.1 to 1.9
- norm_bias: float32 [256], replicated, may hold values from -3 to 3
- qkv_weight: bfloat16 [3, 256, 256], P(None, None, 'ch'), may hold values from -20 to 20
- proj_weight: bfloat16 [256, 256], replicated, may hold values from -1.5 to 1.5
- pool_weight: bfloat16 [256, 512], P(None, 'ch'), may hold values from -0.375 to 0.375
Outputs:
- block_out: bfloat16 [4096, 256], P('pts', 'ch')
- pooled: bfloat16 [1024, 512], P('pts', 'ch')
The draws below stay inside these ranges and needn't reach their ends.
Inputs may be any that keep to these rules, and one draw needn't show every extreme that they name: `owners`: each device's points name every owner at most 128 times; in every draw one owner is named exactly 128 times by the points of every device. `cluster_ids`: cluster ids never fall along the points, every cluster holds one or more points, the points of device i belong to clusters i * 128 - 1 .. i * 128 + 127, and only the first 1 to 3 points of a device (none on device 0) lie in cluster i * 128 - 1; some device has exactly 3 such points. `neighbor_offsets`: offsets -128 and 128 both occur.
All inputs are finite; a program needn't handle non-finite values.
Results may differ from the reference program's by a relative error of at most 0.017.
Values may be sent and summed in bfloat16 or wider, within the bound.
A program may use at most 64 MiB of HBM per device.

```python
import math
import jax
import jax.numpy as jnp
from jax import lax

C = 256
HEADS = 8
HD = 32
PATCH = 1024
P_DEV = 512
POINTS = 4096
CAP = 128
RECV = 1024
NB = 16
K = 27
G = 128
SPILL = 3
M_DEV = 128
M = 1024
N_PTS = 8


def draw_owners(key, part):
    block_count = POINTS // P_DEV
    slot_total = block_count * CAP
    favored = jax.random.randint(jax.random.fold_in(key, 11), (), 0, block_count)
    owner_of = jnp.arange(slot_total, dtype=jnp.int32) // CAP
    slot_ids = jnp.arange(slot_total, dtype=jnp.int32)

    def one_block(block_key):
        bias_key = jax.random.fold_in(block_key, 1)
        score_key = jax.random.fold_in(block_key, 2)
        perm_key = jax.random.fold_in(block_key, 3)
        leaning = jax.random.randint(bias_key, (block_count,), 0, 4)
        noise = jax.random.randint(score_key, (slot_total,), 0, 1 << 14)
        levels = (3 - leaning[owner_of]) * (1 << 14) + noise + 1
        levels = jnp.where(owner_of == favored, 0, levels)
        scores = levels * slot_total + slot_ids
        order = jnp.argsort(scores, stable=True)
        chosen = owner_of[order[:P_DEV]]
        return chosen[jax.random.permutation(perm_key, P_DEV)]
    block_keys = jax.random.split(jax.random.fold_in(key, 12), block_count)
    return jax.vmap(one_block)(block_keys).reshape(POINTS).astype(jnp.int32)


def draw_cluster_ids(key, part):
    block_count = POINTS // P_DEV
    widest = jax.random.randint(jax.random.fold_in(key, 21), (), 1, block_count)
    positions = jnp.arange(P_DEV, dtype=jnp.int32)

    def one_block(block_key, block_index):
        lead_key = jax.random.fold_in(block_key, 1)
        cut_key = jax.random.fold_in(block_key, 2)
        leading = jax.random.randint(lead_key, (), 1, SPILL + 1)
        leading = jnp.where(block_index == widest, SPILL, leading)
        leading = jnp.where(block_index == 0, 0, leading)
        noise = jax.random.randint(cut_key, (P_DEV,), 0, (1 << 30) // P_DEV)
        scores = jnp.where(positions > leading, noise * P_DEV + positions, 2147483647)
        picked = jnp.argsort(scores, stable=True)[:M_DEV - 1]
        cuts = jnp.zeros((P_DEV,), jnp.int32).at[picked].set(1)
        within = jnp.cumsum(cuts)
        return jnp.where(positions < leading, block_index * M_DEV - 1, block_index * M_DEV + within)
    block_keys = jax.random.split(jax.random.fold_in(key, 22), block_count)
    block_ids = jnp.arange(block_count, dtype=jnp.int32)
    return jax.vmap(one_block)(block_keys, block_ids).reshape(POINTS).astype(jnp.int32)


def draw_neighbor_offsets(key, part):
    normal_draw = jax.random.randint(jax.random.fold_in(key, 31), (POINTS, NB), -G, G + 1)
    chosen_rows = jax.random.randint(jax.random.fold_in(key, 32), (2,), 0, POINTS)
    normal_draw = normal_draw.at[chosen_rows[0], 0].set(-G)
    normal_draw = normal_draw.at[chosen_rows[1], 1].set(G)
    return normal_draw.astype(jnp.int32)


def draw_qkv_weight(key, part):
    normal_draw = jax.random.normal(jax.random.fold_in(key, 41), (3, C, C), jnp.float32) * C ** (-0.5)
    normal_draw = jnp.clip(normal_draw, -6.0 * C ** (-0.5), 6.0 * C ** (-0.5))
    return normal_draw.astype(jnp.bfloat16)


def set_ends(array, own_key, least, top_value):
    dims = array.shape
    index_at = [jax.random.randint(jax.random.fold_in(own_key, axis), (), 0, dims[axis]) for axis in range(len(dims))]
    array = array.at[tuple(index_at)].set(least)
    longest = dims.index(max(dims))
    index_at[longest] = (index_at[longest] + 1) % dims[longest]
    return array.at[tuple(index_at)].set(top_value)


def level_of(key, shape, cuts, least, top_value):
    loudness, own = 1.0, jax.random.fold_in(key, 6)
    for axis_at, blocks in cuts:
        heights = jnp.exp(jax.random.uniform(jax.random.fold_in(own, axis_at), (blocks,), jnp.float32, least / len(cuts), top_value / len(cuts)))
        loudness = loudness * jnp.repeat(heights, shape[axis_at] // blocks).reshape([-1 if axis == axis_at else 1 for axis in range(len(shape))])
    return loudness


def bell_draw(rng, shape, scale, most, cuts=(), kind=jnp.bfloat16):
    values = jax.random.normal(rng, shape, jnp.float32) * scale
    if len(cuts) > 0:
        values = level_of(rng, shape, cuts, -0.22, 0.18) * values
    return jnp.clip(values, min=-most, max=most).astype(kind)


def setup_inputs(seed: int = 0) -> dict:
    splits = jax.random.split(jax.random.key(seed), 12)
    return {
        "points_in": bell_draw(splits[0], (POINTS, C), 1.0, 6.0, ((0, 8),)),
        "neighbor_offsets": draw_neighbor_offsets(jax.random.fold_in(splits[11], 71), 0),
        "kernel_ids": set_ends(jax.random.randint(splits[2], (POINTS, NB), 0, K), jax.random.fold_in(splits[2], 1), 0, K - 1).astype(jnp.int32),
        "cluster_ids": draw_cluster_ids(jax.random.fold_in(splits[11], 71), 0),
        "owners": draw_owners(jax.random.fold_in(splits[11], 71), 0),
        "conv_weight": bell_draw(splits[5], (K, C), 0.25, 1.5),
        "norm_gain": jnp.clip(1.0 + 0.18 * jax.random.normal(splits[6], (C,), jnp.float32), 0.1, 1.9),
        "norm_bias": bell_draw(splits[7], (C,), 0.5, 3.0, (), jnp.float32),
        "qkv_weight": draw_qkv_weight(jax.random.fold_in(splits[11], 71), 0),
        "proj_weight": bell_draw(splits[9], (C, C), (C // 16) ** -0.5, 1.5),
        "pool_weight": bell_draw(splits[10], (C, 2 * C), C ** -0.5, 0.375, ((1, 4),)),
    }


def attend_owner(rows_three, live_rows):
    patch_count = RECV // PATCH
    cube = rows_three.astype(jnp.float32).reshape(3, patch_count, PATCH, HEADS, HD)
    queries, key_rows, value_rows = (cube[0], cube[1], cube[2])
    score_scale = 1.0 / math.sqrt(HD)
    scores = jnp.einsum('pqhd,pkhd->phqk', queries, key_rows) * score_scale
    alive_keys = live_rows.reshape(patch_count, 1, 1, PATCH)
    scores = jnp.where(alive_keys, scores, -1e+30)
    row_max = lax.optimization_barrier(jnp.max(scores, axis=-1, keepdims=True))
    weights_f = jnp.exp(scores - row_max)
    denominator = lax.optimization_barrier(jnp.sum(weights_f, axis=-1))
    soft_weights = weights_f.astype(jnp.bfloat16).astype(jnp.float32)
    summed = jnp.einsum('phqk,pkhd->pqhd', soft_weights, value_rows)
    attended = summed / jnp.transpose(denominator, (0, 2, 1))[:, :, :, None]
    return attended.astype(jnp.bfloat16).reshape(RECV, C)

def reference(points_in, neighbor_offsets, kernel_ids, cluster_ids, owners, conv_weight, norm_gain, norm_bias, qkv_weight, proj_weight, pool_weight):
    point_total = points_in.shape[0]
    padded = jnp.pad(points_in, ((G, G), (0, 0)))
    offsets_base = jnp.arange(point_total, dtype=jnp.int32) + G
    kind_ids = jnp.arange(K, dtype=jnp.int32)
    conv = jnp.zeros((point_total, C), jnp.float32)
    for neighbor_slot in range(NB):
        selector = (kernel_ids[:, neighbor_slot][:, None] == kind_ids[None, :]).astype(jnp.bfloat16)
        weights_here = jnp.dot(selector, conv_weight, preferred_element_type=jnp.float32)
        picked = padded[offsets_base + neighbor_offsets[:, neighbor_slot]].astype(jnp.float32)
        conv = conv + weights_here * picked
    residual_rows = (points_in.astype(jnp.float32) + conv).astype(jnp.bfloat16)
    features = residual_rows.astype(jnp.float32)
    average = lax.optimization_barrier(jnp.mean(features, axis=1, keepdims=True))
    centered = features - average
    variance = lax.optimization_barrier(jnp.mean(centered * centered, axis=1, keepdims=True))
    normed_rows = (centered / jnp.sqrt(variance + 1e-05) * norm_gain + norm_bias).astype(jnp.bfloat16)
    qkv = jnp.stack([jnp.dot(normed_rows, qkv_weight[index_t], preferred_element_type=jnp.float32) for index_t in range(3)]).astype(jnp.bfloat16)
    block_count = point_total // P_DEV
    owner_blocks = owners.reshape(block_count, P_DEV)
    peer_ids = jnp.arange(N_PTS, dtype=jnp.int32)
    dest_marks = (owner_blocks[:, :, None] == peer_ids[None, None, :]).astype(jnp.int32)
    earlier_count = jnp.cumsum(dest_marks, axis=1) - dest_marks
    slot_index = lax.optimization_barrier(jnp.sum(earlier_count * dest_marks, axis=2)).reshape(point_total)
    block_ids = jnp.arange(point_total, dtype=jnp.int32) // P_DEV
    position = owners * RECV + block_ids * CAP + slot_index
    source_of = jnp.full((N_PTS * RECV,), point_total, jnp.int32).at[position].set(jnp.arange(point_total, dtype=jnp.int32))
    qkv_ext = jnp.concatenate([qkv, jnp.zeros((3, 1, C), jnp.bfloat16)], axis=1)

    def per_owner(owner_index):
        ids = lax.dynamic_slice_in_dim(source_of, owner_index * RECV, RECV)
        rows_three = qkv_ext[:, ids, :]
        return attend_owner(rows_three, ids < point_total)
    attended = lax.map(per_owner, jnp.arange(N_PTS, dtype=jnp.int32))
    returned = attended.reshape(N_PTS * RECV, C)[position]
    block_out = (residual_rows.astype(jnp.float32) + jnp.dot(returned, proj_weight, preferred_element_type=jnp.float32)).astype(jnp.bfloat16)
    lifted = jnp.dot(block_out, pool_weight, preferred_element_type=jnp.float32)
    cluster_sums = jax.ops.segment_sum(lifted, cluster_ids, num_segments=M)
    cluster_counts = jax.ops.segment_sum(jnp.ones((point_total,), jnp.float32), cluster_ids, num_segments=M)
    pooled = jax.nn.gelu(cluster_sums / cluster_counts[:, None], approximate=False).astype(jnp.bfloat16)
    return (block_out, pooled)
```

```python
import functools
import math

import jax
import jax.numpy as jnp
from jax import lax
from jax.experimental import pallas as pl
from jax.experimental.pallas import tpu as pltpu
from jax.sharding import PartitionSpec as P

HD = 32
G = 128
TILE = 128
CHUNK = 4
QTILE = 256
MESH = pl.DeviceIdType.MESH
BF = jnp.bfloat16
F32 = jnp.float32


def iota(shape, dim):
    return lax.broadcasted_iota(jnp.int32, shape, dim)


def dot(a, b):
    return jnp.dot(a, b, preferred_element_type=F32)


def kernel(
    nodes,
    chans,
    cap,
    x_ref,
    off_ref,
    kid_ref,
    cid_ref,
    own_ref,
    cw_ref,
    gain_ref,
    bias_ref,
    qkvw_ref,
    proj_ref,
    pool_ref,
    full_ref,
    mean_ref,
    xp,
    cw,
    res,
    ext,
    send,
    recv,
    back,
    ret,
    pack,
    gath,
    pw,
    spill_out,
    spill_in,
    halo_send,
    halo_recv,
    fwd_send,
    fwd_recv,
    ret_send,
    ret_recv,
    ch_send,
    ch_recv,
    sp_send,
    sp_recv,
):
    me = lax.axis_index("pts")
    ch = lax.axis_index("ch")
    rows, feats = x_ref.shape
    half = cap // 2
    slots = nodes * cap

    barrier = pltpu.get_barrier_semaphore()

    @pl.loop(1, nodes)
    def _(r):
        pl.semaphore_signal(
            barrier, inc=1, device_id={"pts": lax.rem(me + r, nodes)}, device_id_type=MESH
        )

    for r in range(1, chans):
        pl.semaphore_signal(
            barrier, inc=1, device_id={"ch": lax.rem(ch + r, chans)}, device_id_type=MESH
        )
    pl.semaphore_wait(barrier, nodes - 1 + chans - 1)

    def halo_copy(up):
        if up:
            src, dst, to, at = x_ref.at[pl.ds(rows - G, G)], xp.at[pl.ds(0, G)], me + 1, 0
        else:
            src, dst, to, at = x_ref.at[pl.ds(0, G)], xp.at[pl.ds(rows + G, G)], me - 1, 1
        return pltpu.make_async_remote_copy(
            src_ref=src,
            dst_ref=dst,
            send_sem=halo_send.at[at],
            recv_sem=halo_recv.at[at],
            device_id={"pts": to},
            device_id_type=MESH,
        )

    @pl.when(me < nodes - 1)
    def _():
        halo_copy(True).start()

    @pl.when(me > 0)
    def _():
        halo_copy(False).start()

    @pl.when(me == 0)
    def _():
        xp[pl.ds(0, G), :] = jnp.zeros((G, feats), BF)

    @pl.when(me == nodes - 1)
    def _():
        xp[pl.ds(rows + G, G), :] = jnp.zeros((G, feats), BF)

    xp[pl.ds(G, rows), :] = x_ref[...]
    kinds = cw_ref.shape[0]
    cw[...] = jnp.zeros_like(cw)
    cw[pl.ds(0, kinds), :] = cw_ref[...]

    head_cols = feats // chans
    pw[...] = jnp.zeros_like(pw)
    for c in range(chans):
        part = proj_ref[pl.ds(c * head_cols, head_cols), :]
        pw[0, pl.ds(2 * c * head_cols, head_cols), :] = part
        pw[1, pl.ds((2 * c + 1) * head_cols, head_cols), :] = part

    owner_row = own_ref[...]
    owner_rows = max(nodes, 16)
    marks = iota((owner_rows, rows), 0) == owner_row
    before = (iota((rows, rows), 0) < iota((rows, rows), 1)).astype(F32).astype(BF)
    earlier = dot(marks.astype(F32).astype(BF), before)
    slot_row = jnp.sum(jnp.where(marks, earlier, 0.0), axis=0, keepdims=True).astype(jnp.int32)
    pos_row = owner_row * cap + slot_row
    upper = (slot_row >= half).astype(jnp.int32)
    ret_row = owner_row * half + slot_row - upper * half
    ret_col = jnp.transpose(jnp.broadcast_to(ret_row, (128, rows)).astype(F32)).astype(jnp.int32)
    up_col = jnp.transpose(jnp.broadcast_to(upper, (128, rows)).astype(F32)).astype(jnp.int32)

    gain = gain_ref[...]
    beta = bias_ref[...]
    wqkv = jnp.concatenate(
        [
            qkvw_ref[1],
            jnp.zeros((feats, head_cols), BF),
            qkvw_ref[0],
            qkvw_ref[2],
        ],
        axis=1,
    )
    ones_lane = jnp.logical_and(
        iota((TILE, 4 * head_cols), 1) >= head_cols, iota((TILE, 4 * head_cols), 1) < 2 * head_cols
    )

    def tile(t):
        base = t * TILE
        window = xp[pl.ds(base, TILE + 2 * G), :]
        weights = cw[...]
        offs = off_ref[pl.ds(base, TILE), :] + iota((TILE, off_ref.shape[1]), 0) + G
        kids = kid_ref[pl.ds(base, TILE), :]
        lanes = iota((TILE, TILE + 2 * G), 1)
        kind_lanes = iota((TILE, 128), 1)
        conv = x_ref[pl.ds(base, TILE), :].astype(F32)
        total = jnp.zeros((TILE, feats), F32)
        for first in range(0, off_ref.shape[1], CHUNK):
            pick = jnp.concatenate(
                [
                    (lanes == offs[:, n : n + 1]).astype(F32).astype(BF)
                    for n in range(first, first + CHUNK)
                ],
                axis=0,
            )
            kind = jnp.concatenate(
                [
                    (kind_lanes == kids[:, n : n + 1]).astype(F32).astype(BF)
                    for n in range(first, first + CHUNK)
                ],
                axis=0,
            )
            product = dot(pick, window) * dot(kind, weights)
            for n in range(CHUNK):
                total = total + product[n * TILE : (n + 1) * TILE]
        residual = (conv + total).astype(BF)
        res[pl.ds(base, TILE), :] = residual
        features = residual.astype(F32)
        average = jnp.mean(features, axis=1, keepdims=True)
        centered = features - average
        variance = jnp.mean(centered * centered, axis=1, keepdims=True)
        normed = (centered * lax.rsqrt(variance + 1e-05) * gain + beta).astype(BF)
        projected = jnp.where(ones_lane, 1.0, dot(normed, wqkv))
        ext[pl.ds(base, TILE), :] = projected.astype(BF)

    tiles = rows // TILE
    for t in range(1, tiles - 1):
        tile(t)

    @pl.when(me > 0)
    def _():
        halo_copy(True).wait_recv()

    tile(0)

    @pl.when(me < nodes - 1)
    def _():
        halo_copy(False).wait_recv()

    tile(tiles - 1)

    rows_each = min(slots, 1024)
    for first in range(0, slots, rows_each):
        place = (iota((rows_each, rows), 0) + first == pos_row).astype(F32).astype(BF)
        placed = dot(place, ext[...]).astype(BF)
        send[pl.ds(first // cap, rows_each // cap)] = placed.reshape(rows_each // cap, cap, feats)

    def fwd_copy(r, to):
        return pltpu.make_async_remote_copy(
            src_ref=send.at[to],
            dst_ref=recv.at[me],
            send_sem=fwd_send.at[r],
            recv_sem=fwd_recv.at[r],
            device_id={"pts": to},
            device_id_type=MESH,
        )

    @pl.loop(1, nodes)
    def _(r):
        fwd_copy(r, lax.rem(me + r, nodes)).start()

    recv[me] = send[me]

    @pl.loop(1, nodes)
    def _(r):
        fwd_copy(r, lax.rem(me + r, nodes)).wait_recv()

    everything = recv[...].reshape(slots, feats)
    low = everything[:, : 2 * head_cols]
    lane = iota((slots, 2 * head_cols), 1)
    keys = jnp.where(
        lane < head_cols, low.astype(F32), (low.astype(F32) - 1.0) * 1e30
    ).astype(BF)
    scale = 1.0 / math.sqrt(HD)
    nodes_each = QTILE // cap
    for first in range(0, slots, QTILE):
        query = recv[pl.ds(first // cap, nodes_each)].reshape(QTILE, feats)[:, 2 * head_cols :]
        query = query.astype(F32)
        lane_q = iota((QTILE, 2 * head_cols), 1)
        answer = jnp.zeros((QTILE, 2 * head_cols), F32)
        for h in range(head_cols // HD):
            inside = jnp.logical_and(lane_q >= h * HD, lane_q < (h + 1) * HD)
            one = jnp.where(lane_q == head_cols, 1.0, 0.0)
            query_h = jnp.where(inside, query, one).astype(BF)
            scores = lax.dot_general(
                query_h, keys, (((1,), (1,)), ((), ())), preferred_element_type=F32
            )
            top = jnp.max(scores, axis=1, keepdims=True)
            soft = jnp.exp((scores - top) * scale).astype(BF)
            summed = dot(soft, everything)
            below = summed[:, head_cols : head_cols + 1]
            below = jnp.where(below == 0.0, 1.0, below)
            here = jnp.logical_and(
                lane_q >= head_cols + h * HD, lane_q < head_cols + (h + 1) * HD
            )
            answer = jnp.where(here, summed[:, 2 * head_cols :] / below, answer)
        cube = answer.reshape(nodes_each, cap, 2 * head_cols)
        moved = pltpu.roll(answer, head_cols, 1).reshape(nodes_each, cap, 2 * head_cols)
        lane_b = iota((nodes_each, half, 2 * head_cols), 2)
        both = jnp.where(lane_b < head_cols, moved[:, :half], cube[:, half:])
        back[pl.ds(first // cap, nodes_each)] = both.astype(BF)

    def ret_copy(r, to):
        return pltpu.make_async_remote_copy(
            src_ref=back.at[to],
            dst_ref=ret.at[me],
            send_sem=ret_send.at[r],
            recv_sem=ret_recv.at[r],
            device_id={"pts": to},
            device_id_type=MESH,
        )

    @pl.loop(1, nodes)
    def _(r):
        ret_copy(r, lax.rem(me + r, nodes)).start()

    ret[me] = back[me]

    @pl.loop(1, nodes)
    def _(r):
        ret_copy(r, lax.rem(me + r, nodes)).wait_recv()

    ret_rows = nodes * half
    fetch = (iota((rows, ret_rows), 1) == ret_col[:, :1]).astype(F32).astype(BF)
    fetched = dot(fetch, ret[...].reshape(ret_rows, 2 * head_cols))
    lower_row = iota((rows, 2 * head_cols), 0) >= rows // 2
    same = lower_row == (up_col[:, : 2 * head_cols] > 0)
    fetched = jnp.where(same, fetched, pltpu.roll(fetched, head_cols, 1))
    lane_p = iota((rows // 2, 2 * head_cols), 1)
    packed = jnp.where(lane_p < head_cols, fetched[: rows // 2], fetched[rows // 2 :]).astype(BF)
    pack[...] = packed

    def ch_copy(r):
        return pltpu.make_async_remote_copy(
            src_ref=pack,
            dst_ref=gath.at[ch],
            send_sem=ch_send.at[r],
            recv_sem=ch_recv.at[r],
            device_id={"ch": lax.rem(ch + r, chans)},
            device_id_type=MESH,
        )

    for r in range(1, chans):
        ch_copy(r).start()
    gath[ch] = packed

    count = rows // 4
    local = cid_ref[...] - me * count
    own_marks = (iota((count, rows), 0) == local).astype(F32).astype(BF)
    spill_marks = (jnp.broadcast_to(local, (16, rows)) == -1).astype(F32).astype(BF)

    for r in range(1, chans):
        ch_copy(r).wait_recv()

    wide = jnp.concatenate([gath[c] for c in range(chans)], axis=1)
    for part in range(2):
        at = pl.ds(part * (rows // 2), rows // 2)
        out = res[at, :].astype(F32) + dot(wide, pw[part])
        full_ref[at, :] = out.astype(BF)
    lifted = dot(full_ref[...], pool_ref[...])
    width = lifted.shape[1]
    high = lifted.astype(BF)
    rest = (lifted - high.astype(F32)).astype(BF)
    counted = jnp.concatenate([high, jnp.ones((rows, 128), BF)], axis=1)
    spill = dot(spill_marks, counted)
    spill_rest = dot(spill_marks, rest)
    spill_out[:, :width] = (spill[:, :width] + spill_rest)[:8]
    spill_out[:, width:] = spill[:8, width:]

    def spill_copy():
        return pltpu.make_async_remote_copy(
            src_ref=spill_out,
            dst_ref=spill_in,
            send_sem=sp_send,
            recv_sem=sp_recv,
            device_id={"pts": me - 1},
            device_id_type=MESH,
        )

    @pl.when(me > 0)
    def _():
        spill_copy().start()

    @pl.when(me == nodes - 1)
    def _():
        spill_in[...] = jnp.zeros_like(spill_in)

    mine = dot(own_marks, counted)
    sums = mine[:, :width] + dot(own_marks, rest)
    counts = mine[:, width : width + 128]

    @pl.when(me < nodes - 1)
    def _():
        spill_copy().wait_recv()

    last = iota((count, width), 0) == count - 1
    sums = sums + jnp.where(last, spill_in[0:1, :width], 0.0)
    counts = counts[:, :1] + jnp.where(last, spill_in[0:1, width : width + 1], 0.0)
    mean_ref[...] = sums / counts

    @pl.when(me < nodes - 1)
    def _():
        halo_copy(True).wait_send()

    @pl.when(me > 0)
    def _():
        halo_copy(False).wait_send()

    @pl.loop(1, nodes)
    def _(r):
        fwd_copy(r, lax.rem(me + r, nodes)).wait_send()

    @pl.loop(1, nodes)
    def _(r):
        ret_copy(r, lax.rem(me + r, nodes)).wait_send()

    for r in range(1, chans):
        ch_copy(r).wait_send()

    @pl.when(me > 0)
    def _():
        spill_copy().wait_send()


def shards(
    points_in,
    neighbor_offsets,
    kernel_ids,
    cluster_ids,
    owners,
    conv_weight,
    norm_gain,
    norm_bias,
    qkv_weight,
    proj_weight,
    pool_weight,
):
    rows, feats = points_in.shape
    nodes = lax.axis_size("pts")
    chans = lax.axis_size("ch")
    cap = max(2 * rows // nodes, 32)
    width = pool_weight.shape[1]
    head_cols = qkv_weight.shape[2]
    vmem = pl.BlockSpec(memory_space=pltpu.VMEM)
    full, mean = pl.pallas_call(
        functools.partial(kernel, nodes, chans, cap),
        out_shape=(
            jax.ShapeDtypeStruct((rows, feats), BF),
            jax.ShapeDtypeStruct((rows // 4, width), F32),
        ),
        in_specs=[vmem] * 11,
        out_specs=(vmem, vmem),
        scratch_shapes=[
            pltpu.VMEM((rows + 2 * G, feats), BF),
            pltpu.VMEM((128, feats), BF),
            pltpu.VMEM((rows, feats), BF),
            pltpu.VMEM((rows, feats), BF),
            pltpu.VMEM((nodes, cap, feats), BF),
            pltpu.VMEM((nodes, cap, feats), BF),
            pltpu.VMEM((nodes, cap // 2, 2 * head_cols), BF),
            pltpu.VMEM((nodes, cap // 2, 2 * head_cols), BF),
            pltpu.VMEM((rows // 2, 2 * head_cols), BF),
            pltpu.VMEM((chans, rows // 2, 2 * head_cols), BF),
            pltpu.VMEM((2, 2 * feats, feats), BF),
            pltpu.VMEM((8, width + 128), F32),
            pltpu.VMEM((8, width + 128), F32),
            pltpu.SemaphoreType.DMA((2,)),
            pltpu.SemaphoreType.DMA((2,)),
            pltpu.SemaphoreType.DMA((nodes,)),
            pltpu.SemaphoreType.DMA((nodes,)),
            pltpu.SemaphoreType.DMA((nodes,)),
            pltpu.SemaphoreType.DMA((nodes,)),
            pltpu.SemaphoreType.DMA((chans,)),
            pltpu.SemaphoreType.DMA((chans,)),
            pltpu.SemaphoreType.DMA,
            pltpu.SemaphoreType.DMA,
        ],
        compiler_params=pltpu.CompilerParams(
            collective_id=0, has_side_effects=True, vmem_limit_bytes=48 * 1024 * 1024
        ),
    )(
        points_in,
        neighbor_offsets,
        kernel_ids,
        cluster_ids.reshape(1, rows),
        owners.reshape(1, rows),
        conv_weight,
        norm_gain.reshape(1, feats),
        norm_bias.reshape(1, feats),
        qkv_weight,
        proj_weight,
        pool_weight,
    )
    block_out = lax.dynamic_slice_in_dim(full, lax.axis_index("ch") * head_cols, head_cols, 1)
    pooled = jax.nn.gelu(mean, approximate=False).astype(BF)
    return (block_out, pooled)


def solution(mesh):
    return jax.shard_map(
        shards,
        mesh=mesh,
        in_specs=(
            P("pts", None),
            P("pts", None),
            P("pts", None),
            P("pts"),
            P("pts"),
            P(),
            P(),
            P(),
            P(None, None, "ch"),
            P(),
            P(None, "ch"),
        ),
        out_specs=(P("pts", "ch"), P("pts", "ch")),
        check_vma=False,
    )
```

```python
import functools
import math

import jax
import jax.numpy as jnp
from jax import lax
from jax.experimental import pallas as pl
from jax.experimental.pallas import tpu as pltpu
from jax.sharding import PartitionSpec as P

HD = 32
G = 128
TILE = 128
CHUNK = 4
QTILE = 256
MESH = pl.DeviceIdType.MESH
BF = jnp.bfloat16
F32 = jnp.float32


def iota(shape, dim):
    return lax.broadcasted_iota(jnp.int32, shape, dim)


def dot(a, b):
    return jnp.dot(a, b, preferred_element_type=F32)


def dot_t(a, b):
    return lax.dot_general(a, b, (((1,), (1,)), ((), ())), preferred_element_type=F32)


def each(nodes, count):
    def run(body):
        if nodes <= 8:
            for i in range(count):
                body(i)
        else:
            pl.loop(0, count)(body)

    return run


def kernel(
    nodes,
    chans,
    cap,
    x_ref,
    off_ref,
    kid_ref,
    cid_ref,
    own_ref,
    cw_ref,
    gain_ref,
    bias_ref,
    qkvw_ref,
    proj_ref,
    pool_ref,
    full_ref,
    mean_ref,
    xp,
    cw,
    res,
    ext,
    send,
    recv,
    back,
    ret,
    pack,
    gath,
    pw,
    spill_out,
    spill_in,
    halo_send,
    halo_recv,
    fwd_send,
    fwd_recv,
    ret_send,
    ret_recv,
    ch_send,
    ch_recv,
    sp_send,
    sp_recv,
):
    me = lax.axis_index("pts")
    ch = lax.axis_index("ch")
    rows, feats = x_ref.shape
    half = cap // 2
    slots = nodes * cap

    steps = functools.partial(each, nodes)
    barrier = pltpu.get_barrier_semaphore()

    @pl.loop(1, nodes)
    def _(r):
        pl.semaphore_signal(
            barrier, inc=1, device_id={"pts": lax.rem(me + r, nodes)}, device_id_type=MESH
        )

    for r in range(1, chans):
        pl.semaphore_signal(
            barrier, inc=1, device_id={"ch": lax.rem(ch + r, chans)}, device_id_type=MESH
        )

    xp[pl.ds(G, rows), :] = x_ref[...]
    kinds = cw_ref.shape[0]
    cw[...] = jnp.zeros_like(cw)
    cw[pl.ds(0, kinds), :] = cw_ref[...]
    pl.semaphore_wait(barrier, nodes - 1 + chans - 1)

    def halo_copy(up):
        if up:
            src, dst, to, at = x_ref.at[pl.ds(rows - G, G)], xp.at[pl.ds(0, G)], me + 1, 0
        else:
            src, dst, to, at = x_ref.at[pl.ds(0, G)], xp.at[pl.ds(rows + G, G)], me - 1, 1
        return pltpu.make_async_remote_copy(
            src_ref=src,
            dst_ref=dst,
            send_sem=halo_send.at[at],
            recv_sem=halo_recv.at[at],
            device_id={"pts": to},
            device_id_type=MESH,
        )

    @pl.when(me < nodes - 1)
    def _():
        halo_copy(True).start()

    @pl.when(me > 0)
    def _():
        halo_copy(False).start()

    @pl.when(me == 0)
    def _():
        xp[pl.ds(0, G), :] = jnp.zeros((G, feats), BF)

    @pl.when(me == nodes - 1)
    def _():
        xp[pl.ds(rows + G, G), :] = jnp.zeros((G, feats), BF)

    head_cols = feats // chans
    pw[...] = jnp.zeros_like(pw)
    for c in range(chans):
        part = proj_ref[pl.ds(c * head_cols, head_cols), :]
        pw[0, pl.ds(2 * c * head_cols, head_cols), :] = part
        pw[1, pl.ds((2 * c + 1) * head_cols, head_cols), :] = part

    owner_row = own_ref[...]
    owner_rows = max(nodes, 16)
    marks = iota((owner_rows, rows), 0) == owner_row
    before = (iota((rows, rows), 0) < iota((rows, rows), 1)).astype(F32).astype(BF)
    earlier = dot(marks.astype(F32).astype(BF), before)
    slot_row = jnp.sum(jnp.where(marks, earlier, 0.0), axis=0, keepdims=True).astype(jnp.int32)
    pos_row = owner_row * cap + slot_row
    upper = (slot_row >= half).astype(jnp.int32)
    ret_row = owner_row * half + slot_row - upper * half
    ret_col = jnp.transpose(jnp.broadcast_to(ret_row, (128, rows)).astype(F32)).astype(jnp.int32)
    up_col = jnp.transpose(jnp.broadcast_to(upper, (128, rows)).astype(F32)).astype(jnp.int32)

    gain = gain_ref[...]
    beta = bias_ref[...]
    wqkv = jnp.concatenate(
        [qkvw_ref[1], qkvw_ref[0], qkvw_ref[2], jnp.zeros((head_cols, feats), BF)], axis=0
    )
    ones_lane = iota((TILE, 4 * head_cols), 1) >= 3 * head_cols
    offs_all = jnp.transpose(off_ref[...].astype(F32)).astype(jnp.int32)
    kids_all = jnp.transpose(kid_ref[...].astype(F32)).astype(jnp.int32)

    def tile(t):
        base = t * TILE
        window = xp[pl.ds(base, TILE + 2 * G), :]
        weights = cw[...]
        offs = offs_all[base : base + TILE] + iota((TILE, off_ref.shape[0]), 0) + G
        kids = kids_all[base : base + TILE]
        lanes = iota((TILE, TILE + 2 * G), 1)
        kind_lanes = iota((TILE, 128), 1)
        conv = x_ref[pl.ds(base, TILE), :].astype(F32)
        total = jnp.zeros((TILE, feats), F32)
        for first in range(0, off_ref.shape[0], CHUNK):
            pick = jnp.concatenate(
                [
                    (lanes == offs[:, n : n + 1]).astype(F32).astype(BF)
                    for n in range(first, first + CHUNK)
                ],
                axis=0,
            )
            kind = jnp.concatenate(
                [
                    (kind_lanes == kids[:, n : n + 1]).astype(F32).astype(BF)
                    for n in range(first, first + CHUNK)
                ],
                axis=0,
            )
            product = dot(pick, window) * dot(kind, weights)
            for n in range(CHUNK):
                total = total + product[n * TILE : (n + 1) * TILE]
        residual = (conv + total).astype(BF)
        res[pl.ds(base, TILE), :] = residual
        features = residual.astype(F32)
        average = jnp.mean(features, axis=1, keepdims=True)
        centered = features - average
        variance = jnp.mean(centered * centered, axis=1, keepdims=True)
        normed = (centered * lax.rsqrt(variance + 1e-05) * gain + beta).astype(BF)
        projected = jnp.where(ones_lane, 1.0, dot_t(normed, wqkv))
        ext[pl.ds(base, TILE), :] = projected.astype(BF)

    tiles = rows // TILE
    for t in range(1, tiles - 1):
        tile(t)

    @pl.when(me > 0)
    def _():
        halo_copy(True).wait_recv()

    tile(0)

    @pl.when(me < nodes - 1)
    def _():
        halo_copy(False).wait_recv()

    tile(tiles - 1)

    def fwd_copy(r, to):
        return pltpu.make_async_remote_copy(
            src_ref=send.at[to],
            dst_ref=recv.at[me],
            send_sem=fwd_send.at[r],
            recv_sem=fwd_recv.at[r],
            device_id={"pts": to},
            device_id_type=MESH,
        )

    pair = 2 * head_cols

    def block_for(to):
        place = (iota((cap, rows), 0) + to * cap == pos_row).astype(F32).astype(BF)
        placed = dot(place, ext[...])
        lane = iota((cap, pair), 1)
        dead = jnp.logical_and(lane >= head_cols, placed[:, 3 * head_cols : 3 * head_cols + 1] < 0.5)
        first = jnp.where(dead, 2.0**100, placed[:, :pair])
        second = placed[:, pair:]
        lane_h = iota((half, pair), 1)
        second = jnp.where(lane_h < head_cols, second[:half], pltpu.roll(second[half:], head_cols, 1))
        return first.astype(BF), second.astype(BF)

    @steps(nodes - 1)
    def _(i):
        to = lax.rem(me + i + 1, nodes)
        first, second = block_for(to)
        send[to, pl.ds(0, cap), :] = first
        send[to, pl.ds(cap, half), :] = second
        fwd_copy(i + 1, to).start()

    first, second = block_for(me)
    recv[me, pl.ds(0, cap), :] = first
    recv[me, pl.ds(cap, half), :] = second

    @pl.loop(1, nodes)
    def _(r):
        fwd_copy(r, lax.rem(me + r, nodes)).wait_recv()

    big = 1e29
    low = recv[:, :cap, :].astype(F32).reshape(slots, pair)
    lane = iota((slots, pair), 1)
    gone = low > big
    keys = jnp.where(lane < head_cols, low, jnp.where(gone, -1e30, 0.0)).astype(BF)
    value = recv[:, cap:, :].astype(F32).reshape(nodes * half, pair)
    turned = pltpu.roll(value, head_cols, 1).reshape(nodes, half, pair)
    value = jnp.concatenate([value.reshape(nodes, half, pair), turned], axis=1)
    alive = jnp.where(gone, 0.0, 1.0)
    values = jnp.where(lane < head_cols, value.reshape(slots, pair), alive).astype(BF)
    scale = 1.0 / (math.sqrt(HD) * math.log(2.0))
    group = QTILE // cap
    lane_q = iota((QTILE, pair), 1)

    def ret_copy(r, to):
        return pltpu.make_async_remote_copy(
            src_ref=back.at[to],
            dst_ref=ret.at[me],
            send_sem=ret_send.at[r],
            recv_sem=ret_recv.at[r],
            device_id={"pts": to},
            device_id_type=MESH,
        )

    @steps(nodes // group)
    def _(i):
        whose = [lax.rem(me + i * group + g + 1, nodes) for g in range(group)]
        query = jnp.concatenate([recv[to, pl.ds(0, cap), :] for to in whose], axis=0).astype(F32)
        query = pltpu.roll(jnp.where(query > big, 0.0, query), head_cols, 1)
        answer = jnp.zeros((QTILE, pair), F32)
        for h in range(head_cols // HD):
            inside = jnp.logical_and(lane_q >= h * HD, lane_q < (h + 1) * HD)
            one = jnp.where(lane_q == head_cols, 1.0, 0.0)
            query_h = jnp.where(inside, query, one).astype(BF)
            scores = dot_t(query_h, keys)
            top = jnp.max(scores, axis=1, keepdims=True)
            soft = jnp.exp2((scores - top) * scale).astype(BF)
            summed = dot(soft, values)
            below = summed[:, head_cols : head_cols + 1]
            below = jnp.where(below == 0.0, 1.0, below)
            answer = jnp.where(inside, summed / below, answer)
        moved = pltpu.roll(answer, head_cols, 1)
        lane_b = iota((half, pair), 1)
        for g in range(group):
            at = g * cap
            both = jnp.where(
                lane_b < head_cols, answer[at : at + half], moved[at + half : at + cap]
            ).astype(BF)
            to = whose[g]
            r = i * group + g + 1
            if isinstance(r, int):
                if r == nodes:
                    ret[me] = both
                else:
                    back[to] = both
                    ret_copy(r, to).start()
            else:
                back[to] = both

                @pl.when(r < nodes)
                def _():
                    ret_copy(r, to).start()

                @pl.when(r == nodes)
                def _():
                    ret[me] = back[me]

    @pl.loop(1, nodes)
    def _(r):
        ret_copy(r, lax.rem(me + r, nodes)).wait_recv()

    ret_rows = nodes * half
    fetch = (iota((rows, ret_rows), 1) == ret_col[:, :1]).astype(F32).astype(BF)
    fetched = dot(fetch, ret[...].reshape(ret_rows, 2 * head_cols))
    lower_row = iota((rows, 2 * head_cols), 0) >= rows // 2
    same = lower_row == (up_col[:, : 2 * head_cols] > 0)
    fetched = jnp.where(same, fetched, pltpu.roll(fetched, head_cols, 1))
    lane_p = iota((rows // 2, 2 * head_cols), 1)
    packed = jnp.where(lane_p < head_cols, fetched[: rows // 2], fetched[rows // 2 :]).astype(BF)
    pack[...] = packed

    def ch_copy(r):
        return pltpu.make_async_remote_copy(
            src_ref=pack,
            dst_ref=gath.at[ch],
            send_sem=ch_send.at[r],
            recv_sem=ch_recv.at[r],
            device_id={"ch": lax.rem(ch + r, chans)},
            device_id_type=MESH,
        )

    for r in range(1, chans):
        ch_copy(r).start()
    gath[ch] = packed

    count = rows // 4
    local = cid_ref[...] - me * count
    own_marks = (iota((count, rows), 0) == local).astype(F32).astype(BF)
    spill_marks = (jnp.broadcast_to(local, (16, rows)) == -1).astype(F32).astype(BF)

    for r in range(1, chans):
        ch_copy(r).wait_recv()

    wide = jnp.concatenate([gath[c] for c in range(chans)], axis=1)
    for part in range(2):
        at = pl.ds(part * (rows // 2), rows // 2)
        out = res[at, :].astype(F32) + dot(wide, pw[part])
        res[at, :] = out.astype(BF)
    full = res[...]
    lifted = dot(full, pool_ref[...])
    width = lifted.shape[1]
    high = lifted.astype(BF)
    rest = (lifted - high.astype(F32)).astype(BF)
    counted = jnp.concatenate([high, jnp.ones((rows, 128), BF)], axis=1)
    spill = dot(spill_marks, counted)
    spill_rest = dot(spill_marks, rest)
    spill_out[:, :width] = (spill[:, :width] + spill_rest)[:8]
    spill_out[:, width:] = spill[:8, width:]

    def spill_copy():
        return pltpu.make_async_remote_copy(
            src_ref=spill_out,
            dst_ref=spill_in,
            send_sem=sp_send,
            recv_sem=sp_recv,
            device_id={"pts": me - 1},
            device_id_type=MESH,
        )

    @pl.when(me > 0)
    def _():
        spill_copy().start()

    @pl.when(me == nodes - 1)
    def _():
        spill_in[...] = jnp.zeros_like(spill_in)

    own_lane = iota((head_cols, feats), 1) == iota((head_cols, feats), 0) + ch * head_cols
    full_ref[...] = dot_t(own_lane.astype(F32).astype(BF), full).astype(BF)
    mine = dot(own_marks, counted)
    sums = mine[:, :width] + dot(own_marks, rest)
    counts = mine[:, width : width + 128]

    @pl.when(me < nodes - 1)
    def _():
        spill_copy().wait_recv()

    last = iota((count, width), 0) == count - 1
    sums = sums + jnp.where(last, spill_in[0:1, :width], 0.0)
    counts = counts[:, :1] + jnp.where(last, spill_in[0:1, width : width + 1], 0.0)
    mean_ref[...] = sums / counts

    @pl.when(me < nodes - 1)
    def _():
        halo_copy(True).wait_send()

    @pl.when(me > 0)
    def _():
        halo_copy(False).wait_send()

    @pl.loop(1, nodes)
    def _(r):
        fwd_copy(r, lax.rem(me + r, nodes)).wait_send()

    @pl.loop(1, nodes)
    def _(r):
        ret_copy(r, lax.rem(me + r, nodes)).wait_send()

    for r in range(1, chans):
        ch_copy(r).wait_send()

    @pl.when(me > 0)
    def _():
        spill_copy().wait_send()


def shards(
    points_in,
    neighbor_offsets,
    kernel_ids,
    cluster_ids,
    owners,
    conv_weight,
    norm_gain,
    norm_bias,
    qkv_weight,
    proj_weight,
    pool_weight,
):
    rows, feats = points_in.shape
    nodes = lax.axis_size("pts")
    chans = lax.axis_size("ch")
    cap = max(2 * rows // nodes, 32)
    width = pool_weight.shape[1]
    head_cols = qkv_weight.shape[2]
    vmem = pl.BlockSpec(memory_space=pltpu.VMEM)
    full, mean = pl.pallas_call(
        functools.partial(kernel, nodes, chans, cap),
        out_shape=(
            jax.ShapeDtypeStruct((head_cols, rows), BF),
            jax.ShapeDtypeStruct((rows // 4, width), F32),
        ),
        in_specs=[vmem] * 11,
        out_specs=(vmem, vmem),
        scratch_shapes=[
            pltpu.VMEM((rows + 2 * G, feats), BF),
            pltpu.VMEM((128, feats), BF),
            pltpu.VMEM((rows, feats), BF),
            pltpu.VMEM((rows, feats), BF),
            pltpu.VMEM((nodes, cap + cap // 2, 2 * head_cols), BF),
            pltpu.VMEM((nodes, cap + cap // 2, 2 * head_cols), BF),
            pltpu.VMEM((nodes, cap // 2, 2 * head_cols), BF),
            pltpu.VMEM((nodes, cap // 2, 2 * head_cols), BF),
            pltpu.VMEM((rows // 2, 2 * head_cols), BF),
            pltpu.VMEM((chans, rows // 2, 2 * head_cols), BF),
            pltpu.VMEM((2, 2 * feats, feats), BF),
            pltpu.VMEM((8, width + 128), F32),
            pltpu.VMEM((8, width + 128), F32),
            pltpu.SemaphoreType.DMA((2,)),
            pltpu.SemaphoreType.DMA((2,)),
            pltpu.SemaphoreType.DMA((nodes,)),
            pltpu.SemaphoreType.DMA((nodes,)),
            pltpu.SemaphoreType.DMA((nodes,)),
            pltpu.SemaphoreType.DMA((nodes,)),
            pltpu.SemaphoreType.DMA((chans,)),
            pltpu.SemaphoreType.DMA((chans,)),
            pltpu.SemaphoreType.DMA,
            pltpu.SemaphoreType.DMA,
        ],
        compiler_params=pltpu.CompilerParams(
            collective_id=0, has_side_effects=True, vmem_limit_bytes=48 * 1024 * 1024
        ),
    )(
        points_in,
        neighbor_offsets.T,
        kernel_ids.T,
        cluster_ids.reshape(1, rows),
        owners.reshape(1, rows),
        conv_weight,
        norm_gain.reshape(1, feats),
        norm_bias.reshape(1, feats),
        jnp.transpose(qkv_weight, (0, 2, 1)),
        proj_weight,
        pool_weight,
    )
    block_out = full.T
    pooled = jax.nn.gelu(mean, approximate=False).astype(BF)
    return (block_out, pooled)


def solution(mesh):
    return jax.shard_map(
        shards,
        mesh=mesh,
        in_specs=(
            P("pts", None),
            P("pts", None),
            P("pts", None),
            P("pts"),
            P("pts"),
            P(),
            P(),
            P(),
            P(None, None, "ch"),
            P(),
            P(None, "ch"),
        ),
        out_specs=(P("pts", "ch"), P("pts", "ch")),
        check_vma=False,
    )
```

```python
import functools
import math

import jax
import jax.numpy as jnp
from jax import lax
from jax.experimental import pallas as pl
from jax.experimental.pallas import tpu as pltpu
from jax.sharding import PartitionSpec as P

HD = 32
G = 128
TILE = 128
CHUNK = 4
QTILE = 256
MESH = pl.DeviceIdType.MESH
BF = jnp.bfloat16
F32 = jnp.float32


def iota(shape, dim):
    return lax.broadcasted_iota(jnp.int32, shape, dim)


def dot(a, b):
    return jnp.dot(a, b, preferred_element_type=F32)


def dot_t(a, b):
    return lax.dot_general(a, b, (((1,), (1,)), ((), ())), preferred_element_type=F32)


def each(nodes, count):
    def run(body):
        if nodes <= 8:
            for i in range(count):
                body(i)
        else:
            pl.loop(0, count)(body)

    return run


def kernel(
    nodes,
    chans,
    cap,
    x_ref,
    off_in,
    kid_in,
    cid_in,
    own_in,
    cw_in,
    gain_in,
    bias_in,
    qkvw_in,
    proj_in,
    pool_in,
    full_ref,
    mean_ref,
    off_ref,
    kid_ref,
    cid_ref,
    own_ref,
    cw_ref,
    gain_ref,
    bias_ref,
    qkvw_ref,
    proj_ref,
    pool_ref,
    in_sem,
    xp,
    cw,
    res,
    ext,
    send,
    recv,
    back,
    ret,
    pack,
    gath,
    pw,
    next_res,
    next_pack,
    next_cid,
    halo_send,
    halo_recv,
    fwd_send,
    fwd_recv,
    ret_send,
    ret_recv,
    ch_send,
    ch_recv,
    next_send,
    next_recv,
    pack_send,
    pack_recv,
):
    me = lax.axis_index("pts")
    ch = lax.axis_index("ch")
    rows, feats = x_ref.shape
    half = cap // 2
    slots = nodes * cap

    steps = functools.partial(each, nodes)
    loads = [
        pltpu.make_async_copy(src, dst, in_sem.at[i])
        for i, (src, dst) in enumerate(
            [
                (own_in, own_ref),
                (x_ref, xp.at[pl.ds(G, rows)]),
                (cw_in, cw_ref),
                (off_in, off_ref),
                (kid_in, kid_ref),
                (gain_in, gain_ref),
                (bias_in, bias_ref),
                (qkvw_in, qkvw_ref),
                (proj_in, proj_ref),
                (pool_in, pool_ref),
                (cid_in, cid_ref),
            ]
        )
    ]
    for load in loads:
        load.start()
    barrier = pltpu.get_barrier_semaphore()

    @pl.loop(1, nodes)
    def _(r):
        pl.semaphore_signal(
            barrier, inc=1, device_id={"pts": lax.rem(me + r, nodes)}, device_id_type=MESH
        )

    for r in range(1, chans):
        pl.semaphore_signal(
            barrier, inc=1, device_id={"ch": lax.rem(ch + r, chans)}, device_id_type=MESH
        )

    for by in (1, nodes - 1):
        for r in range(1, chans):
            beside = {"pts": lax.rem(me + by, nodes), "ch": lax.rem(ch + r, chans)}
            pl.semaphore_signal(barrier, inc=1, device_id=beside, device_id_type=MESH)

    kinds = cw_ref.shape[0]
    cw[...] = jnp.zeros_like(cw)
    pw[...] = jnp.zeros_like(pw)
    pl.semaphore_wait(barrier, nodes - 1 + 3 * (chans - 1))

    def next_copy(at):
        src, dst = ((cid_in, next_cid), (res.at[pl.ds(0, 16)], next_res))[at]
        return pltpu.make_async_remote_copy(
            src_ref=src,
            dst_ref=dst,
            send_sem=next_send.at[at],
            recv_sem=next_recv.at[at],
            device_id={"pts": me - 1},
            device_id_type=MESH,
        )

    def pack_copy(r):
        return pltpu.make_async_remote_copy(
            src_ref=pack.at[pl.ds(0, 16)],
            dst_ref=next_pack.at[ch],
            send_sem=pack_send.at[r],
            recv_sem=pack_recv.at[r],
            device_id={"pts": me - 1, "ch": lax.rem(ch + r, chans)},
            device_id_type=MESH,
        )

    def halo_copy(up):
        if up:
            src, dst, to, at = x_ref.at[pl.ds(rows - G, G)], xp.at[pl.ds(0, G)], me + 1, 0
        else:
            src, dst, to, at = x_ref.at[pl.ds(0, G)], xp.at[pl.ds(rows + G, G)], me - 1, 1
        return pltpu.make_async_remote_copy(
            src_ref=src,
            dst_ref=dst,
            send_sem=halo_send.at[at],
            recv_sem=halo_recv.at[at],
            device_id={"pts": to},
            device_id_type=MESH,
        )

    @pl.when(me < nodes - 1)
    def _():
        halo_copy(True).start()

    @pl.when(me > 0)
    def _():
        halo_copy(False).start()
        next_copy(0).start()

    @pl.when(me == 0)
    def _():
        xp[pl.ds(0, G), :] = jnp.zeros((G, feats), BF)

    @pl.when(me == nodes - 1)
    def _():
        xp[pl.ds(rows + G, G), :] = jnp.zeros((G, feats), BF)
        next_res[...] = jnp.zeros_like(next_res)
        next_pack[...] = jnp.zeros_like(next_pack)
        next_cid[...] = jnp.full_like(next_cid, -1)

    head_cols = feats // chans
    loads[0].wait()

    owner_row = own_ref[...]
    owner_rows = max(nodes, 16)
    marks = iota((owner_rows, rows), 0) == owner_row
    before = (iota((rows, rows), 0) < iota((rows, rows), 1)).astype(F32).astype(BF)
    earlier = dot(marks.astype(F32).astype(BF), before)
    slot_row = jnp.sum(jnp.where(marks, earlier, 0.0), axis=0, keepdims=True).astype(jnp.int32)
    pos_row = owner_row * cap + slot_row
    upper = (slot_row >= half).astype(jnp.int32)
    ret_row = owner_row * half + slot_row - upper * half
    ret_col = jnp.transpose(jnp.broadcast_to(ret_row, (128, rows)).astype(F32)).astype(jnp.int32)
    up_col = jnp.transpose(jnp.broadcast_to(upper, (128, rows)).astype(F32)).astype(jnp.int32)

    for load in loads[1:8]:
        load.wait()
    cw[pl.ds(0, kinds), :] = cw_ref[...]
    gain = gain_ref[...]
    beta = bias_ref[...]
    wqkv = jnp.concatenate(
        [qkvw_ref[1], qkvw_ref[0], qkvw_ref[2], jnp.zeros((head_cols, feats), BF)], axis=0
    )
    ones_lane = iota((TILE, 4 * head_cols), 1) >= 3 * head_cols
    offs_all = jnp.transpose(off_ref[...].astype(F32)).astype(jnp.int32)
    kids_all = jnp.transpose(kid_ref[...].astype(F32)).astype(jnp.int32)

    one_b = jnp.array(1.0, BF)
    zero_b = jnp.array(0.0, BF)

    def tile(t):
        base = t * TILE
        window = xp[pl.ds(base, TILE + 2 * G), :]
        weights = cw[...]
        middle = TILE // 2
        offs = offs_all[base : base + TILE] + iota((TILE, off_ref.shape[0]), 0) - middle
        offs = offs.astype(F32).astype(BF)
        kids = kids_all[base : base + TILE].astype(F32).astype(BF)
        lanes = (iota((TILE, TILE + 2 * G), 1) - (G + middle)).astype(F32).astype(BF)
        kind_lanes = iota((TILE, 128), 1).astype(F32).astype(BF)
        conv = xp[pl.ds(base + G, TILE), :].astype(F32)
        total = jnp.zeros((TILE, feats), F32)
        for first in range(0, off_ref.shape[0], CHUNK):
            pick = jnp.concatenate(
                [
                    jnp.where(lanes == offs[:, n : n + 1], one_b, zero_b)
                    for n in range(first, first + CHUNK)
                ],
                axis=0,
            )
            kind = jnp.concatenate(
                [
                    jnp.where(kind_lanes == kids[:, n : n + 1], one_b, zero_b)
                    for n in range(first, first + CHUNK)
                ],
                axis=0,
            )
            product = dot(pick, window) * dot(kind, weights)
            for n in range(CHUNK):
                total = total + product[n * TILE : (n + 1) * TILE]
        residual = (conv + total).astype(BF)
        res[pl.ds(base, TILE), :] = residual
        features = residual.astype(F32)
        average = jnp.mean(features, axis=1, keepdims=True)
        centered = features - average
        variance = jnp.mean(centered * centered, axis=1, keepdims=True)
        normed = (centered * lax.rsqrt(variance + 1e-05) * gain + beta).astype(BF)
        projected = jnp.where(ones_lane, 1.0, dot_t(normed, wqkv))
        ext[pl.ds(base, TILE), :] = projected.astype(BF)

    tiles = rows // TILE
    for t in range(1, tiles - 1):
        tile(t)

    @pl.when(me > 0)
    def _():
        halo_copy(True).wait_recv()

    tile(0)

    @pl.when(me > 0)
    def _():
        next_copy(1).start()

    @pl.when(me < nodes - 1)
    def _():
        halo_copy(False).wait_recv()

    tile(tiles - 1)

    def fwd_copy(r, to):
        return pltpu.make_async_remote_copy(
            src_ref=send.at[to],
            dst_ref=recv.at[me],
            send_sem=fwd_send.at[r],
            recv_sem=fwd_recv.at[r],
            device_id={"pts": to},
            device_id_type=MESH,
        )

    pair = 2 * head_cols

    def block_for(to):
        place = (iota((cap, rows), 0) + to * cap == pos_row).astype(F32).astype(BF)
        placed = dot(place, ext[...])
        lane = iota((cap, pair), 1)
        dead = jnp.logical_and(lane >= head_cols, placed[:, 3 * head_cols : 3 * head_cols + 1] < 0.5)
        first = jnp.where(dead, 2.0**100, placed[:, :pair])
        second = placed[:, pair:]
        lane_h = iota((half, pair), 1)
        second = jnp.where(lane_h < head_cols, second[:half], pltpu.roll(second[half:], head_cols, 1))
        return first.astype(BF), second.astype(BF)

    @steps(nodes - 1)
    def _(i):
        to = lax.rem(me + i + 1, nodes)
        first, second = block_for(to)
        send[to, pl.ds(0, cap), :] = first
        send[to, pl.ds(cap, half), :] = second
        fwd_copy(i + 1, to).start()

    for load in loads[8:]:
        load.wait()
    for c in range(chans):
        part = proj_ref[pl.ds(c * head_cols, head_cols), :]
        pw[0, pl.ds(2 * c * head_cols, head_cols), :] = part
        pw[1, pl.ds((2 * c + 1) * head_cols, head_cols), :] = part

    first, second = block_for(me)
    recv[me, pl.ds(0, cap), :] = first
    recv[me, pl.ds(cap, half), :] = second

    @pl.loop(1, nodes)
    def _(r):
        fwd_copy(r, lax.rem(me + r, nodes)).wait_recv()

    big = 1e29
    low = recv[:, :cap, :].astype(F32).reshape(slots, pair)
    lane = iota((slots, pair), 1)
    gone = low > big
    keys = jnp.where(lane < head_cols, low, jnp.where(gone, -1e30, 0.0)).astype(BF)
    value = recv[:, cap:, :].astype(F32).reshape(nodes * half, pair)
    turned = pltpu.roll(value, head_cols, 1).reshape(nodes, half, pair)
    value = jnp.concatenate([value.reshape(nodes, half, pair), turned], axis=1)
    alive = jnp.where(gone, 0.0, 1.0)
    values = jnp.where(lane < head_cols, value.reshape(slots, pair), alive).astype(BF)
    scale = 1.0 / (math.sqrt(HD) * math.log(2.0))
    group = QTILE // cap
    lane_q = iota((QTILE, pair), 1)

    def ret_copy(r, to):
        return pltpu.make_async_remote_copy(
            src_ref=back.at[to],
            dst_ref=ret.at[me],
            send_sem=ret_send.at[r],
            recv_sem=ret_recv.at[r],
            device_id={"pts": to},
            device_id_type=MESH,
        )

    @steps(nodes // group)
    def _(i):
        whose = [lax.rem(me + i * group + g + 1, nodes) for g in range(group)]
        query = jnp.concatenate([recv[to, pl.ds(0, cap), :] for to in whose], axis=0).astype(F32)
        query = pltpu.roll(jnp.where(query > big, 0.0, query), head_cols, 1)
        answer = jnp.zeros((QTILE, pair), F32)
        for h in range(head_cols // HD):
            inside = jnp.logical_and(lane_q >= h * HD, lane_q < (h + 1) * HD)
            one = jnp.where(lane_q == head_cols, 1.0, 0.0)
            query_h = jnp.where(inside, query, one).astype(BF)
            scores = dot_t(query_h, keys)
            top = jnp.max(scores, axis=1, keepdims=True)
            soft = jnp.exp2((scores - top) * scale).astype(BF)
            summed = dot(soft, values)
            below = summed[:, head_cols : head_cols + 1]
            below = jnp.where(below == 0.0, 1.0, below)
            answer = jnp.where(inside, summed / below, answer)
        moved = pltpu.roll(answer, head_cols, 1)
        lane_b = iota((half, pair), 1)
        for g in range(group):
            at = g * cap
            both = jnp.where(
                lane_b < head_cols, answer[at : at + half], moved[at + half : at + cap]
            ).astype(BF)
            to = whose[g]
            r = i * group + g + 1
            if isinstance(r, int):
                if r == nodes:
                    ret[me] = both
                else:
                    back[to] = both
                    ret_copy(r, to).start()
            else:
                back[to] = both

                @pl.when(r < nodes)
                def _():
                    ret_copy(r, to).start()

                @pl.when(r == nodes)
                def _():
                    ret[me] = back[me]

    @pl.loop(1, nodes)
    def _(r):
        ret_copy(r, lax.rem(me + r, nodes)).wait_recv()

    ret_rows = nodes * half
    fetch = (iota((rows, ret_rows), 1) == ret_col[:, :1]).astype(F32).astype(BF)
    fetched = dot(fetch, ret[...].reshape(ret_rows, 2 * head_cols))
    lower_row = iota((rows, 2 * head_cols), 0) >= rows // 2
    same = lower_row == (up_col[:, : 2 * head_cols] > 0)
    fetched = jnp.where(same, fetched, pltpu.roll(fetched, head_cols, 1))
    lane_p = iota((rows // 2, 2 * head_cols), 1)
    packed = jnp.where(lane_p < head_cols, fetched[: rows // 2], fetched[rows // 2 :]).astype(BF)
    pack[...] = packed

    def ch_copy(r):
        return pltpu.make_async_remote_copy(
            src_ref=pack,
            dst_ref=gath.at[ch],
            send_sem=ch_send.at[r],
            recv_sem=ch_recv.at[r],
            device_id={"ch": lax.rem(ch + r, chans)},
            device_id_type=MESH,
        )

    for r in range(1, chans):
        ch_copy(r).start()

    @pl.when(me > 0)
    def _():
        for r in range(chans):
            pack_copy(r).start()

    gath[ch] = packed

    count = rows // 4
    local = cid_ref[...] - me * count
    own_marks = (iota((count, rows), 0) == local).astype(F32).astype(BF)

    for r in range(1, chans):
        ch_copy(r).wait_recv()

    wide = jnp.concatenate([gath[c] for c in range(chans)], axis=1)
    for part in range(2):
        at = pl.ds(part * (rows // 2), rows // 2)
        out = res[at, :].astype(F32) + dot(wide, pw[part])
        ext[at, :] = out.astype(BF)
    full = ext[...]
    own_lane = iota((head_cols, feats), 1) == iota((head_cols, feats), 0) + ch * head_cols
    full_ref[...] = dot_t(own_lane.astype(F32).astype(BF), full).astype(BF)

    def summed_up(marks, some):
        lifted = dot(some, pool_ref[...])
        high = lifted.astype(BF)
        rest = (lifted - high.astype(F32)).astype(BF)
        counted = jnp.concatenate([high, jnp.ones((some.shape[0], 128), BF)], axis=1)
        both = dot(marks, counted)
        width = lifted.shape[1]
        return both[:, :width] + dot(marks, rest), both[:, width : width + 1]

    sums, counts = summed_up(own_marks, full)

    @pl.when(me < nodes - 1)
    def _():
        for at in range(2):
            next_copy(at).wait_recv()
        for r in range(chans):
            pack_copy(r).wait_recv()

    next_local = next_cid[...][:, :16] - me * count
    next_marks = (iota((count, 16), 0) == next_local).astype(F32).astype(BF)
    next_wide = jnp.concatenate([next_pack[c] for c in range(chans)], axis=1)
    next_full = (next_res[...].astype(F32) + dot(next_wide, pw[0])).astype(BF)
    more, more_counts = summed_up(next_marks, next_full)
    mean_ref[...] = (sums + more) / (counts + more_counts)

    @pl.when(me < nodes - 1)
    def _():
        halo_copy(True).wait_send()

    @pl.when(me > 0)
    def _():
        halo_copy(False).wait_send()

    @pl.loop(1, nodes)
    def _(r):
        fwd_copy(r, lax.rem(me + r, nodes)).wait_send()

    @pl.loop(1, nodes)
    def _(r):
        ret_copy(r, lax.rem(me + r, nodes)).wait_send()

    for r in range(1, chans):
        ch_copy(r).wait_send()

    @pl.when(me > 0)
    def _():
        for at in range(2):
            next_copy(at).wait_send()
        for r in range(chans):
            pack_copy(r).wait_send()


def shards(
    points_in,
    neighbor_offsets,
    kernel_ids,
    cluster_ids,
    owners,
    conv_weight,
    norm_gain,
    norm_bias,
    qkv_weight,
    proj_weight,
    pool_weight,
):
    rows, feats = points_in.shape
    nodes = lax.axis_size("pts")
    chans = lax.axis_size("ch")
    cap = max(2 * rows // nodes, 32)
    width = pool_weight.shape[1]
    head_cols = qkv_weight.shape[2]
    vmem = pl.BlockSpec(memory_space=pltpu.VMEM)
    hbm = pl.BlockSpec(memory_space=pltpu.HBM)
    near = pltpu.VMEM
    full, mean = pl.pallas_call(
        functools.partial(kernel, nodes, chans, cap),
        out_shape=(
            jax.ShapeDtypeStruct((head_cols, rows), BF),
            jax.ShapeDtypeStruct((rows // 4, width), F32),
        ),
        in_specs=[hbm] * 11,
        out_specs=(vmem, vmem),
        scratch_shapes=[
            near(neighbor_offsets.shape[::-1], jnp.int32),
            near(kernel_ids.shape[::-1], jnp.int32),
            near((1, rows), jnp.int32),
            near((1, rows), jnp.int32),
            near(conv_weight.shape, BF),
            near((1, feats), F32),
            near((1, feats), F32),
            near((3, head_cols, feats), BF),
            near(proj_weight.shape, BF),
            near(pool_weight.shape, BF),
            pltpu.SemaphoreType.DMA((11,)),
            pltpu.VMEM((rows + 2 * G, feats), BF),
            pltpu.VMEM((128, feats), BF),
            pltpu.VMEM((rows, feats), BF),
            pltpu.VMEM((rows, feats), BF),
            pltpu.VMEM((nodes, cap + cap // 2, 2 * head_cols), BF),
            pltpu.VMEM((nodes, cap + cap // 2, 2 * head_cols), BF),
            pltpu.VMEM((nodes, cap // 2, 2 * head_cols), BF),
            pltpu.VMEM((nodes, cap // 2, 2 * head_cols), BF),
            pltpu.VMEM((rows // 2, 2 * head_cols), BF),
            pltpu.VMEM((chans, rows // 2, 2 * head_cols), BF),
            pltpu.VMEM((2, 2 * feats, feats), BF),
            pltpu.VMEM((16, feats), BF),
            pltpu.VMEM((chans, 16, 2 * head_cols), BF),
            pltpu.VMEM((1, rows), jnp.int32),
            pltpu.SemaphoreType.DMA((2,)),
            pltpu.SemaphoreType.DMA((2,)),
            pltpu.SemaphoreType.DMA((nodes,)),
            pltpu.SemaphoreType.DMA((nodes,)),
            pltpu.SemaphoreType.DMA((nodes,)),
            pltpu.SemaphoreType.DMA((nodes,)),
            pltpu.SemaphoreType.DMA((chans,)),
            pltpu.SemaphoreType.DMA((chans,)),
            pltpu.SemaphoreType.DMA((2,)),
            pltpu.SemaphoreType.DMA((2,)),
            pltpu.SemaphoreType.DMA((chans,)),
            pltpu.SemaphoreType.DMA((chans,)),
        ],
        compiler_params=pltpu.CompilerParams(
            collective_id=0, has_side_effects=True, vmem_limit_bytes=64 * 1024 * 1024
        ),
    )(
        points_in,
        neighbor_offsets.T,
        kernel_ids.T,
        cluster_ids.reshape(1, rows),
        owners.reshape(1, rows),
        conv_weight,
        norm_gain.reshape(1, feats),
        norm_bias.reshape(1, feats),
        jnp.transpose(qkv_weight, (0, 2, 1)),
        proj_weight,
        pool_weight,
    )
    block_out = full.T
    pooled = jax.nn.gelu(mean, approximate=False).astype(BF)
    return (block_out, pooled)


def solution(mesh):
    return jax.shard_map(
        shards,
        mesh=mesh,
        in_specs=(
            P("pts", None),
            P("pts", None),
            P("pts", None),
            P("pts"),
            P("pts"),
            P(),
            P(),
            P(),
            P(None, None, "ch"),
            P(),
            P(None, "ch"),
        ),
        out_specs=(P("pts", "ch"), P("pts", "ch")),
        check_vma=False,
    )
```

```python
import functools
import math

import jax
import jax.numpy as jnp
from jax import lax
from jax.experimental import pallas as pl
from jax.experimental.pallas import tpu as pltpu
from jax.sharding import PartitionSpec as P

HD = 32
G = 128
TILE = 128
CHUNK = 4
QTILE = 256
MESH = pl.DeviceIdType.MESH
BF = jnp.bfloat16
F32 = jnp.float32


def iota(shape, dim):
    return lax.broadcasted_iota(jnp.int32, shape, dim)


def dot(a, b):
    return jnp.dot(a, b, preferred_element_type=F32)


def dot_t(a, b):
    return lax.dot_general(a, b, (((1,), (1,)), ((), ())), preferred_element_type=F32)


def each(nodes, count):
    def run(body):
        if nodes <= 8:
            for i in range(count):
                body(i)
        else:
            pl.loop(0, count)(body)

    return run


def kernel(
    nodes,
    chans,
    cap,
    x_ref,
    off_in,
    kid_in,
    cid_in,
    own_in,
    cw_in,
    gain_in,
    bias_in,
    qkvw_in,
    proj_in,
    pool_in,
    full_out,
    pooled_out,
    full_ref,
    pooled_ref,
    out_sem,
    off_ref,
    kid_ref,
    cid_ref,
    own_ref,
    cw_ref,
    gain_ref,
    bias_ref,
    qkvw_ref,
    proj_ref,
    pool_ref,
    in_sem,
    xp,
    cw,
    res,
    ext,
    send,
    recv,
    back,
    ret,
    pack,
    gath,
    pw,
    next_res,
    next_pack,
    next_cid,
    halo_send,
    halo_recv,
    fwd_send,
    fwd_recv,
    ret_send,
    ret_recv,
    ch_send,
    ch_recv,
    next_send,
    next_recv,
    pack_send,
    pack_recv,
):
    me = lax.axis_index("pts")
    ch = lax.axis_index("ch")
    rows, feats = x_ref.shape
    half = cap // 2
    slots = nodes * cap

    steps = functools.partial(each, nodes)
    far = sorted(range(1, nodes), key=lambda r: abs(2 * r - nodes)) + [nodes]

    def distance(i):
        return far[i] if isinstance(i, int) else i + 1

    loads = [
        pltpu.make_async_copy(src, dst, in_sem.at[i])
        for i, (src, dst) in enumerate(
            [
                (own_in, own_ref),
                (x_ref, xp.at[pl.ds(G, rows)]),
                (cw_in, cw_ref),
                (off_in, off_ref),
                (kid_in, kid_ref),
                (gain_in, gain_ref),
                (bias_in, bias_ref),
                (qkvw_in, qkvw_ref),
                (proj_in, proj_ref),
                (pool_in, pool_ref),
                (cid_in, cid_ref),
            ]
        )
    ]
    for load in loads:
        load.start()
    barrier = pltpu.get_barrier_semaphore()

    @pl.loop(1, nodes)
    def _(r):
        pl.semaphore_signal(
            barrier, inc=1, device_id={"pts": lax.rem(me + r, nodes)}, device_id_type=MESH
        )

    for r in range(1, chans):
        pl.semaphore_signal(
            barrier, inc=1, device_id={"ch": lax.rem(ch + r, chans)}, device_id_type=MESH
        )

    for by in (1, nodes - 1):
        for r in range(1, chans):
            beside = {"pts": lax.rem(me + by, nodes), "ch": lax.rem(ch + r, chans)}
            pl.semaphore_signal(barrier, inc=1, device_id=beside, device_id_type=MESH)

    kinds = cw_ref.shape[0]
    cw[...] = jnp.zeros_like(cw)
    pw[...] = jnp.zeros_like(pw)
    pl.semaphore_wait(barrier, nodes - 1 + 3 * (chans - 1))

    def next_copy(at):
        src, dst = ((cid_in, next_cid), (res.at[pl.ds(0, 16)], next_res))[at]
        return pltpu.make_async_remote_copy(
            src_ref=src,
            dst_ref=dst,
            send_sem=next_send.at[at],
            recv_sem=next_recv.at[at],
            device_id={"pts": me - 1},
            device_id_type=MESH,
        )

    def pack_copy(r):
        return pltpu.make_async_remote_copy(
            src_ref=pack.at[pl.ds(0, 16)],
            dst_ref=next_pack.at[ch],
            send_sem=pack_send.at[r],
            recv_sem=pack_recv.at[r],
            device_id={"pts": me - 1, "ch": lax.rem(ch + r, chans)},
            device_id_type=MESH,
        )

    def halo_copy(up):
        if up:
            src, dst, to, at = x_ref.at[pl.ds(rows - G, G)], xp.at[pl.ds(0, G)], me + 1, 0
        else:
            src, dst, to, at = x_ref.at[pl.ds(0, G)], xp.at[pl.ds(rows + G, G)], me - 1, 1
        return pltpu.make_async_remote_copy(
            src_ref=src,
            dst_ref=dst,
            send_sem=halo_send.at[at],
            recv_sem=halo_recv.at[at],
            device_id={"pts": to},
            device_id_type=MESH,
        )

    @pl.when(me < nodes - 1)
    def _():
        halo_copy(True).start()

    @pl.when(me > 0)
    def _():
        halo_copy(False).start()
        next_copy(0).start()

    @pl.when(me == 0)
    def _():
        xp[pl.ds(0, G), :] = jnp.zeros((G, feats), BF)

    @pl.when(me == nodes - 1)
    def _():
        xp[pl.ds(rows + G, G), :] = jnp.zeros((G, feats), BF)
        next_res[...] = jnp.zeros_like(next_res)
        next_pack[...] = jnp.zeros_like(next_pack)
        next_cid[...] = jnp.full_like(next_cid, -1)

    head_cols = feats // chans
    loads[0].wait()

    owner_row = own_ref[...]
    owner_rows = max(nodes, 16)
    marks = iota((owner_rows, rows), 0) == owner_row
    before = (iota((rows, rows), 0) < iota((rows, rows), 1)).astype(F32).astype(BF)
    earlier = dot(marks.astype(F32).astype(BF), before)
    slot_row = jnp.sum(jnp.where(marks, earlier, 0.0), axis=0, keepdims=True).astype(jnp.int32)
    pos_row = owner_row * cap + slot_row
    upper = (slot_row >= half).astype(jnp.int32)
    ret_row = owner_row * half + slot_row - upper * half
    ret_col = jnp.transpose(jnp.broadcast_to(ret_row, (128, rows)).astype(F32)).astype(jnp.int32)
    up_col = jnp.transpose(jnp.broadcast_to(upper, (128, rows)).astype(F32)).astype(jnp.int32)

    for load in loads[1:8]:
        load.wait()
    cw[pl.ds(0, kinds), :] = cw_ref[...]
    gain = gain_ref[...]
    beta = bias_ref[...]
    wqkv = jnp.concatenate(
        [qkvw_ref[1], qkvw_ref[0], qkvw_ref[2], jnp.zeros((head_cols, feats), BF)], axis=0
    )
    ones_lane = iota((TILE, 4 * head_cols), 1) >= 3 * head_cols
    offs_all = jnp.transpose(off_ref[...].astype(F32)).astype(jnp.int32)
    kids_all = jnp.transpose(kid_ref[...].astype(F32)).astype(jnp.int32)

    one_b = jnp.array(1.0, BF)
    zero_b = jnp.array(0.0, BF)

    def tile(t):
        base = t * TILE
        window = xp[pl.ds(base, TILE + 2 * G), :]
        weights = cw[...]
        middle = TILE // 2
        offs = offs_all[base : base + TILE] + iota((TILE, off_ref.shape[0]), 0) - middle
        offs = offs.astype(F32).astype(BF)
        kids = kids_all[base : base + TILE].astype(F32).astype(BF)
        lanes = (iota((TILE, TILE + 2 * G), 1) - (G + middle)).astype(F32).astype(BF)
        kind_lanes = iota((TILE, 128), 1).astype(F32).astype(BF)
        conv = xp[pl.ds(base + G, TILE), :].astype(F32)
        total = jnp.zeros((TILE, feats), F32)
        for first in range(0, off_ref.shape[0], CHUNK):
            pick = jnp.concatenate(
                [
                    jnp.where(lanes == offs[:, n : n + 1], one_b, zero_b)
                    for n in range(first, first + CHUNK)
                ],
                axis=0,
            )
            kind = jnp.concatenate(
                [
                    jnp.where(kind_lanes == kids[:, n : n + 1], one_b, zero_b)
                    for n in range(first, first + CHUNK)
                ],
                axis=0,
            )
            product = dot(pick, window) * dot(kind, weights)
            for n in range(CHUNK):
                total = total + product[n * TILE : (n + 1) * TILE]
        residual = (conv + total).astype(BF)
        res[pl.ds(base, TILE), :] = residual
        features = residual.astype(F32)
        average = jnp.mean(features, axis=1, keepdims=True)
        centered = features - average
        variance = jnp.mean(centered * centered, axis=1, keepdims=True)
        normed = (centered * lax.rsqrt(variance + 1e-05) * gain + beta).astype(BF)
        projected = jnp.where(ones_lane, 1.0, dot_t(normed, wqkv))
        ext[pl.ds(base, TILE), :] = projected.astype(BF)

    tiles = rows // TILE
    for t in range(1, tiles - 1):
        tile(t)

    @pl.when(me > 0)
    def _():
        halo_copy(True).wait_recv()

    tile(0)

    @pl.when(me > 0)
    def _():
        next_copy(1).start()

    @pl.when(me < nodes - 1)
    def _():
        halo_copy(False).wait_recv()

    tile(tiles - 1)

    def fwd_copy(r, to):
        return pltpu.make_async_remote_copy(
            src_ref=send.at[to],
            dst_ref=recv.at[me],
            send_sem=fwd_send.at[r],
            recv_sem=fwd_recv.at[r],
            device_id={"pts": to},
            device_id_type=MESH,
        )

    pair = 2 * head_cols

    def block_for(to):
        place = (iota((cap, rows), 0) + to * cap == pos_row).astype(F32).astype(BF)
        placed = dot(place, ext[...])
        lane = iota((cap, pair), 1)
        dead = jnp.logical_and(lane >= head_cols, placed[:, 3 * head_cols : 3 * head_cols + 1] < 0.5)
        first = jnp.where(dead, 2.0**100, placed[:, :pair])
        second = placed[:, pair:]
        lane_h = iota((half, pair), 1)
        second = jnp.where(lane_h < head_cols, second[:half], pltpu.roll(second[half:], head_cols, 1))
        return first.astype(BF), second.astype(BF)

    @steps(nodes - 1)
    def _(i):
        r = distance(i)
        to = lax.rem(me + r, nodes)
        first, second = block_for(to)
        send[to, pl.ds(0, cap), :] = first
        send[to, pl.ds(cap, half), :] = second
        fwd_copy(r, to).start()

    for load in loads[8:]:
        load.wait()
    for c in range(chans):
        part = proj_ref[pl.ds(c * head_cols, head_cols), :]
        pw[0, pl.ds(2 * c * head_cols, head_cols), :] = part
        pw[1, pl.ds((2 * c + 1) * head_cols, head_cols), :] = part

    first, second = block_for(me)
    recv[me, pl.ds(0, cap), :] = first
    recv[me, pl.ds(cap, half), :] = second

    @pl.loop(1, nodes)
    def _(r):
        fwd_copy(r, lax.rem(me + r, nodes)).wait_recv()

    big = 1e29
    low = recv[:, :cap, :].astype(F32).reshape(slots, pair)
    lane = iota((slots, pair), 1)
    gone = low > big
    keys = jnp.where(lane < head_cols, low, jnp.where(gone, -1e30, 0.0)).astype(BF)
    value = recv[:, cap:, :].astype(F32).reshape(nodes * half, pair)
    turned = pltpu.roll(value, head_cols, 1).reshape(nodes, half, pair)
    value = jnp.concatenate([value.reshape(nodes, half, pair), turned], axis=1)
    alive = jnp.where(gone, 0.0, 1.0)
    values = jnp.where(lane < head_cols, value.reshape(slots, pair), alive).astype(BF)
    scale = 1.0 / (math.sqrt(HD) * math.log(2.0))
    group = QTILE // cap
    lane_q = iota((QTILE, pair), 1)

    def ret_copy(r, to):
        return pltpu.make_async_remote_copy(
            src_ref=back.at[to],
            dst_ref=ret.at[me],
            send_sem=ret_send.at[r],
            recv_sem=ret_recv.at[r],
            device_id={"pts": to},
            device_id_type=MESH,
        )

    @steps(nodes // group)
    def _(i):
        whose = [lax.rem(me + distance(i * group + g), nodes) for g in range(group)]
        query = jnp.concatenate([recv[to, pl.ds(0, cap), :] for to in whose], axis=0).astype(F32)
        query = pltpu.roll(jnp.where(query > big, 0.0, query), head_cols, 1)
        answer = jnp.zeros((QTILE, pair), F32)
        for h in range(head_cols // HD):
            inside = jnp.logical_and(lane_q >= h * HD, lane_q < (h + 1) * HD)
            one = jnp.where(lane_q == head_cols, 1.0, 0.0)
            query_h = jnp.where(inside, query, one).astype(BF)
            scores = dot_t(query_h, keys)
            top = jnp.max(scores, axis=1, keepdims=True)
            soft = jnp.exp2((scores - top) * scale).astype(BF)
            summed = dot(soft, values)
            below = summed[:, head_cols : head_cols + 1]
            below = jnp.where(below == 0.0, 1.0, below)
            answer = jnp.where(inside, summed / below, answer)
        moved = pltpu.roll(answer, head_cols, 1)
        lane_b = iota((half, pair), 1)
        for g in range(group):
            at = g * cap
            both = jnp.where(
                lane_b < head_cols, answer[at : at + half], moved[at + half : at + cap]
            ).astype(BF)
            to = whose[g]
            r = distance(i * group + g)
            if isinstance(r, int):
                if r == nodes:
                    ret[me] = both
                else:
                    back[to] = both
                    ret_copy(r, to).start()
            else:
                back[to] = both

                @pl.when(r < nodes)
                def _():
                    ret_copy(r, to).start()

                @pl.when(r == nodes)
                def _():
                    ret[me] = back[me]

    @pl.loop(1, nodes)
    def _(r):
        ret_copy(r, lax.rem(me + r, nodes)).wait_recv()

    ret_rows = nodes * half
    fetch = (iota((rows, ret_rows), 1) == ret_col[:, :1]).astype(F32).astype(BF)
    fetched = dot(fetch, ret[...].reshape(ret_rows, 2 * head_cols))
    lower_row = iota((rows, 2 * head_cols), 0) >= rows // 2
    same = lower_row == (up_col[:, : 2 * head_cols] > 0)
    fetched = jnp.where(same, fetched, pltpu.roll(fetched, head_cols, 1))
    lane_p = iota((rows // 2, 2 * head_cols), 1)
    packed = jnp.where(lane_p < head_cols, fetched[: rows // 2], fetched[rows // 2 :]).astype(BF)
    pack[...] = packed

    def ch_copy(r):
        return pltpu.make_async_remote_copy(
            src_ref=pack,
            dst_ref=gath.at[ch],
            send_sem=ch_send.at[r],
            recv_sem=ch_recv.at[r],
            device_id={"ch": lax.rem(ch + r, chans)},
            device_id_type=MESH,
        )

    for r in range(1, chans):
        ch_copy(r).start()

    @pl.when(me > 0)
    def _():
        for r in range(chans):
            pack_copy(r).start()

    gath[ch] = packed

    count = rows // 4
    local = cid_ref[...] - me * count
    own_marks = (iota((count, rows), 0) == local).astype(F32).astype(BF)

    for r in range(1, chans):
        ch_copy(r).wait_recv()

    wide = jnp.concatenate([gath[c] for c in range(chans)], axis=1)
    for part in range(2):
        at = pl.ds(part * (rows // 2), rows // 2)
        out = res[at, :].astype(F32) + dot(wide, pw[part])
        ext[at, :] = out.astype(BF)
    full = ext[...]
    own_lane = iota((head_cols, feats), 1) == iota((head_cols, feats), 0) + ch * head_cols
    full_ref[...] = dot_t(own_lane.astype(F32).astype(BF), full).astype(BF)
    full_copy = pltpu.make_async_copy(full_ref, full_out, out_sem.at[0])
    full_copy.start()

    def summed_up(marks, some):
        lifted = dot(some, pool_ref[...])
        high = lifted.astype(BF)
        rest = (lifted - high.astype(F32)).astype(BF)
        counted = jnp.concatenate([high, jnp.ones((some.shape[0], 128), BF)], axis=1)
        both = dot(marks, counted)
        width = lifted.shape[1]
        return both[:, :width] + dot(marks, rest), both[:, width : width + 1]

    sums, counts = summed_up(own_marks, full)

    @pl.when(me < nodes - 1)
    def _():
        for at in range(2):
            next_copy(at).wait_recv()
        for r in range(chans):
            pack_copy(r).wait_recv()

    next_local = next_cid[...][:, :16] - me * count
    next_marks = (iota((count, 16), 0) == next_local).astype(F32).astype(BF)
    next_wide = jnp.concatenate([next_pack[c] for c in range(chans)], axis=1)
    next_full = (next_res[...].astype(F32) + dot(next_wide, pw[0])).astype(BF)
    more, more_counts = summed_up(next_marks, next_full)
    mean = (sums + more) / (counts + more_counts)
    pooled_ref[...] = (mean * (1.0 + lax.erf(mean * math.sqrt(0.5))) * 0.5).astype(BF)
    pooled_copy = pltpu.make_async_copy(pooled_ref, pooled_out, out_sem.at[1])
    pooled_copy.start()

    full_copy.wait()
    pooled_copy.wait()

    @pl.when(me < nodes - 1)
    def _():
        halo_copy(True).wait_send()

    @pl.when(me > 0)
    def _():
        halo_copy(False).wait_send()

    @pl.loop(1, nodes)
    def _(r):
        fwd_copy(r, lax.rem(me + r, nodes)).wait_send()

    @pl.loop(1, nodes)
    def _(r):
        ret_copy(r, lax.rem(me + r, nodes)).wait_send()

    for r in range(1, chans):
        ch_copy(r).wait_send()

    @pl.when(me > 0)
    def _():
        for at in range(2):
            next_copy(at).wait_send()
        for r in range(chans):
            pack_copy(r).wait_send()


def shards(
    points_in,
    neighbor_offsets,
    kernel_ids,
    cluster_ids,
    owners,
    conv_weight,
    norm_gain,
    norm_bias,
    qkv_weight,
    proj_weight,
    pool_weight,
):
    rows, feats = points_in.shape
    nodes = lax.axis_size("pts")
    chans = lax.axis_size("ch")
    cap = max(2 * rows // nodes, 32)
    width = pool_weight.shape[1]
    head_cols = qkv_weight.shape[2]
    hbm = pl.BlockSpec(memory_space=pltpu.HBM)
    near = pltpu.VMEM
    full, pooled = pl.pallas_call(
        functools.partial(kernel, nodes, chans, cap),
        out_shape=(
            jax.ShapeDtypeStruct((head_cols, rows), BF),
            jax.ShapeDtypeStruct((rows // 4, width), BF),
        ),
        in_specs=[hbm] * 11,
        out_specs=(hbm, hbm),
        scratch_shapes=[
            near((head_cols, rows), BF),
            near((rows // 4, width), BF),
            pltpu.SemaphoreType.DMA((2,)),
            near(neighbor_offsets.shape[::-1], jnp.int32),
            near(kernel_ids.shape[::-1], jnp.int32),
            near((1, rows), jnp.int32),
            near((1, rows), jnp.int32),
            near(conv_weight.shape, BF),
            near((1, feats), F32),
            near((1, feats), F32),
            near((3, head_cols, feats), BF),
            near(proj_weight.shape, BF),
            near(pool_weight.shape, BF),
            pltpu.SemaphoreType.DMA((11,)),
            pltpu.VMEM((rows + 2 * G, feats), BF),
            pltpu.VMEM((128, feats), BF),
            pltpu.VMEM((rows, feats), BF),
            pltpu.VMEM((rows, feats), BF),
            pltpu.VMEM((nodes, cap + cap // 2, 2 * head_cols), BF),
            pltpu.VMEM((nodes, cap + cap // 2, 2 * head_cols), BF),
            pltpu.VMEM((nodes, cap // 2, 2 * head_cols), BF),
            pltpu.VMEM((nodes, cap // 2, 2 * head_cols), BF),
            pltpu.VMEM((rows // 2, 2 * head_cols), BF),
            pltpu.VMEM((chans, rows // 2, 2 * head_cols), BF),
            pltpu.VMEM((2, 2 * feats, feats), BF),
            pltpu.VMEM((16, feats), BF),
            pltpu.VMEM((chans, 16, 2 * head_cols), BF),
            pltpu.VMEM((1, rows), jnp.int32),
            pltpu.SemaphoreType.DMA((2,)),
            pltpu.SemaphoreType.DMA((2,)),
            pltpu.SemaphoreType.DMA((nodes,)),
            pltpu.SemaphoreType.DMA((nodes,)),
            pltpu.SemaphoreType.DMA((nodes,)),
            pltpu.SemaphoreType.DMA((nodes,)),
            pltpu.SemaphoreType.DMA((chans,)),
            pltpu.SemaphoreType.DMA((chans,)),
            pltpu.SemaphoreType.DMA((2,)),
            pltpu.SemaphoreType.DMA((2,)),
            pltpu.SemaphoreType.DMA((chans,)),
            pltpu.SemaphoreType.DMA((chans,)),
        ],
        compiler_params=pltpu.CompilerParams(
            collective_id=0, has_side_effects=True, vmem_limit_bytes=64 * 1024 * 1024
        ),
    )(
        points_in,
        neighbor_offsets.T,
        kernel_ids.T,
        cluster_ids.reshape(1, rows),
        owners.reshape(1, rows),
        conv_weight,
        norm_gain.reshape(1, feats),
        norm_bias.reshape(1, feats),
        jnp.transpose(qkv_weight, (0, 2, 1)),
        proj_weight,
        pool_weight,
    )
    block_out = full.T
    return (block_out, pooled)


def solution(mesh):
    return jax.shard_map(
        shards,
        mesh=mesh,
        in_specs=(
            P("pts", None),
            P("pts", None),
            P("pts", None),
            P("pts"),
            P("pts"),
            P(),
            P(),
            P(),
            P(None, None, "ch"),
            P(),
            P(None, "ch"),
        ),
        out_specs=(P("pts", "ch"), P("pts", "ch")),
        check_vma=False,
    )
```
